32 devices in a mesh: row: 4 (over x, core), col: 8 (over z, y).
Axes of the slice: x: 2, y: 2, z: 4, core: 2. Of those that a mesh axis runs over, the one named last changes fastest.
Arguments:
- local_ops: bfloat16 [8, 8, 2048, 2048], P('row', 'col'), as said below
- start_vecs: float32 [8, 8, 1024, 128], P('row', 'col'), may hold values from -6 to 6
- multipliers: float32 [8, 8, 1024, 128], P('row', 'col'), may hold values from -6 to 6
- dual_rhs: float32 [8, 8, 1024, 128], P('row', 'col'), may hold values from -48 to 48
- mode_traces: bfloat16 [8, 8, 6, 2048], P('row', 'col'), may hold values from -0.1875 to 0.1875
- coarse_mult: float32 [8, 8, 6, 128], P('row', 'col'), may hold values from -6 to 6
- coarse_rhs: float32 [8, 8, 6, 128], P('row', 'col'), may hold values from -6 to 6
- face_size: int32 [8, 8, 2], P('row', 'col'), may hold values from 0 to 512, as said below
- contact: int32 [8, 8, 2], P('row', 'col'), may hold values 0 or 1
- mode_count: int32 [8, 8], P('row', 'col'), may hold values from 0 to 6
Outputs:
- new_multipliers: float32 [8, 8, 1024, 128], P('row', 'col')
- power_vectors: float32 [8, 8, 1024, 128], P('row', 'col')
- column_norms: float32 [128], replicated
- new_coarse: float32 [8, 8, 6, 128], P('row', 'col')
The draws below stay inside these ranges and needn't reach their ends.
Inputs may be any that keep to these rules, and one draw needn't show every extreme that they name: face_size[r, c, 0] counts the live multipliers of the face between subdomains (r, c) and (r, c + 1), face_size[r, c, 1] of the face between (r, c) and (r + 1, c): a multiple of 128 from 128 to 512 for inner faces, 0 for faces on the grid's last column or last row. `local_ops`: each local operator is symmetric.
All inputs are finite; a program needn't handle non-finite values. No bound on the sum of `contact` on one device may be relied on, other than what follows from the above.
Results may differ from the reference program's by a relative error of at most 0.0007.
The reference program's roundings to bfloat16 on the way count: a program that leaves them out, or rounds other values in their place, can miss the bound.
Values may be sent and summed in bfloat16 or wider, within the bound.
A program may use at most 128 MiB of HBM per device.

```python
import math
import jax
import jax.numpy as jnp
from jax import lax

M = 2048
FS = 512
GRAIN = 128
K = 6
NV = 128
ITERS = 4
GR = 8
GC = 8


def draw_local_ops(key, part):
    key = jax.random.fold_in(key, 11)

    def single(subdomain):
        sub_key = jax.random.fold_in(key, subdomain)
        noise_key, diag_key = jax.random.split(sub_key)
        noise = jax.random.normal(noise_key, (M, M), jnp.float32)
        lowest, highest = (2.5, 25.0)
        symmetric = (noise + noise.T) * (0.70710678 / math.sqrt(M))
        diagonal = jnp.exp(jax.random.uniform(diag_key, (M,), jnp.float32, math.log(lowest), math.log(highest)))
        grid_row = subdomain // GC
        grid_col = subdomain % GC
        factor = jnp.power(3.0, (grid_row + grid_col).astype(jnp.float32) / (GR + GC - 2))
        return ((symmetric + jnp.diag(diagonal)) * factor).astype(jnp.bfloat16)
    return lax.map(single, jnp.arange(GR * GC, dtype=jnp.int32)).reshape(GR, GC, M, M)


def draw_face_size(key, part):
    key = jax.random.fold_in(key, 23)
    widths = jax.random.randint(key, (GR, GC, 2), 1, FS // GRAIN + 1) * GRAIN
    grid_row = lax.broadcasted_iota(jnp.int32, (GR, GC, 2), 0)
    grid_col = lax.broadcasted_iota(jnp.int32, (GR, GC, 2), 1)
    face_slot = lax.broadcasted_iota(jnp.int32, (GR, GC, 2), 2)
    on_edge = (face_slot == 0) & (grid_col == GC - 1) | (face_slot == 1) & (grid_row == GR - 1)
    corner = (grid_row == 0) & (grid_col == 0) & (face_slot == 0)
    sizes = jnp.where(corner, FS, widths)
    return jnp.where(on_edge, 0, sizes).astype(jnp.int32)


def set_ends(array, key, low, high):
    longest = array.shape.index(max(array.shape))
    spots = []
    for shift in (0, 1):
        where = [jax.random.randint(jax.random.fold_in(key, axis), (), 0, length) for axis, length in enumerate(array.shape)]
        where[longest] = (where[longest] + shift) % array.shape[longest]
        spots.append(tuple(where))
    return array.at[spots[0]].set(low).at[spots[1]].set(high)


def block_scale(stream_key, dims, cuts, smallest, largest):
    gain = 1.0
    for dim, blocks in cuts:
        steps = jax.random.uniform(jax.random.fold_in(jax.random.fold_in(stream_key, 6), dim), (blocks,), jnp.float32, smallest / len(cuts), largest / len(cuts))
        gain = gain * jnp.repeat(jnp.exp(steps), dims[dim] // blocks).reshape((-1,) + (1,) * (len(dims) - 1 - dim))
    return gain


def normal_values(key, shape, width, bound, cuts=(), kind=jnp.bfloat16):
    array = jax.random.normal(key, shape, jnp.float32) * width
    if len(cuts) > 0:
        array = block_scale(key, shape, cuts, -0.22, 0.18) * array
    return jnp.clip(array, min=-bound, max=bound).astype(kind)


def setup_inputs(seed: int = 0) -> dict:
    key_of = jax.random.split(jax.random.key(seed), 11)
    local_ops = draw_local_ops(jax.random.fold_in(key_of[10], 71), 0)
    start_vecs = normal_values(key_of[1], (GR, GC, 2 * FS, NV), 1.0, 6.0, ((0, 4), (1, 8)), jnp.float32)
    multipliers = normal_values(key_of[2], (GR, GC, 2 * FS, NV), 1.0, 6.0, ((0, 4), (1, 8)), jnp.float32)
    dual_rhs = normal_values(key_of[3], (GR, GC, 2 * FS, NV), 8.0, 48.0, ((0, 4), (1, 8)), jnp.float32)
    mode_traces = normal_values(key_of[4], (GR, GC, K, M), (M // 2) ** -0.5, 0.1875, ((0, 4), (1, 8)))
    coarse_mult = normal_values(key_of[5], (GR, GC, K, NV), 1.0, 6.0, ((0, 4), (1, 8)), jnp.float32)
    coarse_rhs = normal_values(key_of[6], (GR, GC, K, NV), 1.0, 6.0, ((0, 4), (1, 8)), jnp.float32)
    face_size = draw_face_size(jax.random.fold_in(key_of[10], 71), 0)
    contact = set_ends((jax.random.randint(key_of[8], (GR, GC, 2), 0, 2) < 1).astype(jnp.int32), jax.random.fold_in(key_of[8], 1), 0, 1)
    mode_count = set_ends(jax.random.randint(key_of[9], (GR, GC), 0, K + 1), jax.random.fold_in(key_of[9], 1), 0, K).astype(jnp.int32)
    return {"local_ops": local_ops, "start_vecs": start_vecs, "multipliers": multipliers, "dual_rhs": dual_rhs, "mode_traces": mode_traces, "coarse_mult": coarse_mult, "coarse_rhs": coarse_rhs, "face_size": face_size, "contact": contact, "mode_count": mode_count}


EPSILON = 1e-06

def shift_grid(field, grid_axis, offset):
    extent = field.shape[grid_axis]
    zero_edge = jnp.zeros_like(lax.slice_in_dim(field, 0, 1, axis=grid_axis))
    if offset == 1:
        return jnp.concatenate([zero_edge, lax.slice_in_dim(field, 0, extent - 1, axis=grid_axis)], grid_axis)
    return jnp.concatenate([lax.slice_in_dim(field, 1, extent, axis=grid_axis), zero_edge], grid_axis)

def operate(operators, owned, live_mask, coarse):
    slot_width = owned.shape[2] // 2
    east_faces = owned[:, :, :slot_width]
    south_faces = owned[:, :, slot_width:]
    signed = jnp.concatenate([-shift_grid(east_faces, 1, 1), east_faces, -shift_grid(south_faces, 0, 1), south_faces], 2)
    grid_rows, grid_cols, order_size, columns = signed.shape
    product = lax.map(lambda operands: jnp.dot(operands[0], operands[1], preferred_element_type=jnp.float32), (operators.reshape(grid_rows * grid_cols, order_size, order_size), signed.reshape(grid_rows * grid_cols, order_size, columns)))
    product = product.reshape(grid_rows, grid_cols, order_size, columns)
    coarse_gap = None
    if coarse is not None:
        traces, coarse_mult, coarse_rhs, mode_live = coarse
        dual_part = signed[..., columns - coarse_mult.shape[-1]:].astype(jnp.float32)
        coarse_gap = (jnp.einsum('rckm,rcmn->rckn', traces, dual_part, precision=lax.Precision.HIGHEST) - coarse_rhs) * mode_live
        coarse_part = jnp.einsum('rckm,rckn->rcmn', traces, jnp.concatenate([coarse_mult, coarse_gap], 3), precision=lax.Precision.HIGHEST)
        product = jnp.concatenate([product, coarse_part], 3)
    west_part = product[:, :, :slot_width]
    east_part = product[:, :, slot_width:2 * slot_width]
    north_part = product[:, :, 2 * slot_width:3 * slot_width]
    south_part = product[:, :, 3 * slot_width:]
    assembled = jnp.concatenate([east_part - shift_grid(west_part, 1, -1), south_part - shift_grid(north_part, 0, -1)], 2)
    return (assembled * live_mask, coarse_gap)

def reference(local_ops, start_vecs, multipliers, dual_rhs, mode_traces, coarse_mult, coarse_rhs, face_size, contact, mode_count):
    grid_rows, grid_cols, owned_len, columns = start_vecs.shape
    slot_width = owned_len // 2
    modes = mode_traces.shape[2]
    position = lax.broadcasted_iota(jnp.int32, (grid_rows, grid_cols, 2, slot_width), 3)
    live_mask = (position < face_size[:, :, :, None]).astype(jnp.float32).reshape(grid_rows, grid_cols, owned_len, 1)
    contact_mask = jnp.broadcast_to(contact[:, :, :, None] > 0, (grid_rows, grid_cols, 2, slot_width)).reshape(grid_rows, grid_cols, owned_len, 1)
    mode_live = (lax.broadcasted_iota(jnp.int32, (grid_rows, grid_cols, modes), 2) < mode_count[:, :, None]).astype(jnp.float32)[:, :, :, None]
    traces = mode_traces.astype(jnp.float32) * mode_live
    vectors = start_vecs * live_mask
    previous_sums = jnp.zeros((columns,), jnp.float32)
    last_sums = jnp.zeros((columns,), jnp.float32)
    for sweep in range(ITERS):
        images, unused = operate(local_ops, vectors.astype(jnp.bfloat16), live_mask, None)
        previous_sums = last_sums
        last_sums = lax.optimization_barrier(jnp.sum(images * images, axis=(0, 1, 2)))
        vectors = images
    column_norms = jnp.sqrt((last_sums + EPSILON) / (previous_sums + EPSILON))
    vectors = vectors / jnp.sqrt(last_sums + EPSILON)
    penalty = jnp.max(column_norms)
    step_length = 1.9 / penalty
    base = multipliers * live_mask
    masked_mult = coarse_mult * mode_live
    assembled, coarse_gap = operate(local_ops, base.astype(jnp.bfloat16), live_mask, (traces, masked_mult, coarse_rhs, mode_live))
    grad = assembled[..., :columns] + assembled[..., columns:2 * columns] + penalty * assembled[..., 2 * columns:] - dual_rhs * live_mask
    trial = base - step_length * grad
    new_multipliers = jnp.where(contact_mask, jnp.maximum(trial, 0.0), trial) * live_mask
    new_coarse = masked_mult + penalty * coarse_gap
    return (new_multipliers, vectors, column_norms, new_coarse)
```

```python
import functools
import jax
import jax.numpy as jnp
from jax import lax
from jax.experimental import pallas as pl
from jax.experimental.pallas import tpu as pltpu
from jax.sharding import PartitionSpec as P

ITERS = 4
EPSILON = 1e-06
LANES = 128
GRAIN = 128
MODE_ROWS = 8
TOP = 32767.0
TINY = 1e-30
WEST, EAST, NORTH, SOUTH = 0, 1, 2, 3
SIGN = (-1.0, 1.0, -1.0, 1.0)
MESH = pl.DeviceIdType.MESH


def kernel(
    mesh_rows,
    mesh_cols,
    ops_hbm,
    start_ref,
    mult_ref,
    rhs_ref,
    traces_ref,
    coarse_mult_ref,
    coarse_rhs_ref,
    size_ref,
    contact_ref,
    count_ref,
    new_mult_ref,
    power_ref,
    norms_ref,
    new_coarse_ref,
    ops,
    signed,
    first_out,
    own_prod,
    base_prod,
    base_grad,
    own_diag,
    far_diag,
    info_out,
    info_in,
    code_out,
    code_in,
    scale_out,
    scale_in,
    modes_out,
    modes_in,
    traces_own,
    live,
    sums_out,
    sums_col,
    sums_row,
    load_sems,
    first_send,
    first_recv,
    info_send,
    info_recv,
    code_send,
    code_recv,
    scale_send,
    scale_recv,
    modes_send,
    modes_recv,
    col_send,
    col_recv,
    row_send,
    row_recv,
):
    blocks, order_size, _ = ops.shape
    face = order_size // 4
    grains = face // GRAIN
    modes = traces_ref.shape[1]
    base_index = ITERS
    row = lax.axis_index("row")
    col = lax.axis_index("col")

    loads = [
        pltpu.make_async_copy(ops_hbm.at[s], ops.at[s], load_sems.at[s]) for s in range(blocks)
    ]
    for load in loads:
        load.start()

    barrier = pltpu.get_barrier_semaphore()
    for step in range(1, mesh_cols):
        pl.semaphore_signal(
            barrier,
            inc=1,
            device_id=(row, lax.rem(col + step, mesh_cols)),
            device_id_type=MESH,
        )
    for step in range(1, mesh_rows):
        pl.semaphore_signal(
            barrier,
            inc=1,
            device_id=(lax.rem(row + step, mesh_rows), col),
            device_id_type=MESH,
        )

    links = []
    for s in range(blocks):
        links.append((s, blocks + s, s, WEST, col > 0, (row, col - 1)))
        links.append((blocks + s, s, s, EAST, col < mesh_cols - 1, (row, col + 1)))
    north_slot, south_slot = 2 * blocks, 2 * blocks + 1
    links.append((north_slot, south_slot, 0, NORTH, row > 0, (row - 1, col)))
    links.append(
        (south_slot, north_slot, blocks - 1, SOUTH, row < mesh_rows - 1, (row + 1, col))
    )
    owner_links = [link for link in links if link[3] in (EAST, SOUTH)]
    far_links = [link for link in links if link[3] in (WEST, NORTH)]

    def rows_of(side):
        return pl.ds(side * face, face)

    def remote(src, dst, send_sem, recv_sem, device):
        return pltpu.make_async_remote_copy(
            src_ref=src,
            dst_ref=dst,
            send_sem=send_sem,
            recv_sem=recv_sem,
            device_id=device,
            device_id_type=MESH,
        )

    def first_copy(link):
        here, there, s, side, _, device = link
        far_s = s if side == EAST else 0
        return remote(
            first_out.at[here],
            signed.at[far_s, rows_of(side - 1), :],
            first_send.at[here],
            first_recv.at[there],
            device,
        )

    def first_arrival(link):
        here, _, s, side, _, device = link
        return remote(
            first_out.at[here],
            signed.at[s, rows_of(side), :],
            first_send.at[here],
            first_recv.at[here],
            device,
        )

    def plain_copy(src, dst, send_sems, recv_sems, link, index=None):
        here, there, device = link[0], link[1], link[5]
        if index is None:
            return remote(
                src.at[here], dst.at[there], send_sems.at[here], recv_sems.at[there], device
            )
        return remote(
            src.at[index, here],
            dst.at[index, there],
            send_sems.at[index, here],
            recv_sems.at[index, there],
            device,
        )

    def arrival(src, dst, send_sems, recv_sems, link, index=None):
        here, device = link[0], link[5]
        if index is None:
            return remote(
                src.at[here], dst.at[here], send_sems.at[here], recv_sems.at[here], device
            )
        return remote(
            src.at[index, here],
            dst.at[index, here],
            send_sems.at[index, here],
            recv_sems.at[index, here],
            device,
        )

    info_bufs = (info_out, info_in, info_send, info_recv)
    code_bufs = (code_out, code_in, code_send, code_recv)
    scale_bufs = (scale_out, scale_in, scale_send, scale_recv)
    modes_bufs = (modes_out, modes_in, modes_send, modes_recv)

    grain_start = lax.broadcasted_iota(jnp.int32, (8, LANES), 0) * GRAIN
    for s in range(blocks):
        for half in range(2):
            live[s, half] = (grain_start < size_ref[s, half]).astype(jnp.float32)
    for s in range(blocks):
        for half, side in ((0, EAST), (1, SOUTH)):
            for grain in range(grains):
                mask = live[s, half, grain : grain + 1, :]
                src = pl.ds(half * face + grain * GRAIN, GRAIN)
                dst = pl.ds(side * face + grain * GRAIN, GRAIN)
                signed[s, dst, 0:LANES] = (start_ref[s, src, :] * mask).astype(jnp.bfloat16)
                signed[s, dst, LANES : 2 * LANES] = (mult_ref[s, src, :] * mask).astype(
                    jnp.bfloat16
                )
    for link in owner_links:
        here, _, s, side = link[:4]
        first_out[here] = -signed[s, rows_of(side), :]
    for s in range(1, blocks):
        signed[s, rows_of(NORTH), :] = -signed[s - 1, rows_of(SOUTH), :]

    pl.semaphore_wait(barrier, mesh_cols - 1 + mesh_rows - 1)
    for link in owner_links:

        @pl.when(link[4])
        def _(link=link):
            first_copy(link).start()

    for link in far_links:

        @pl.when(jnp.logical_not(link[4]))
        def _(link=link):
            signed[link[2], rows_of(link[3]), :] = jnp.zeros((face, 2 * LANES), jnp.bfloat16)

    for link in owner_links:

        @pl.when(jnp.logical_not(link[4]))
        def _(link=link):
            here, _, s, side = link[:4]
            modes_in[here] = jnp.zeros(modes_in.shape[1:], jnp.float32)
            out_rows = pl.ds((side // 2) * face, face)
            power_ref[s, out_rows, :] = jnp.zeros((face, LANES), jnp.float32)
            base_grad[s, out_rows, :] = jnp.zeros((face, LANES), jnp.float32)

    traces_own[...] = jnp.zeros_like(traces_own)
    coarse_live = []
    for s in range(blocks):
        mask = (
            lax.broadcasted_iota(jnp.int32, (modes, LANES), 0) < count_ref[s, 0]
        ).astype(jnp.float32)
        coarse_live.append(mask)
        mode_mask = (
            lax.broadcasted_iota(jnp.int32, (modes, order_size), 0) < count_ref[s, 0]
        ).astype(jnp.float32)
        traces_own[s, 0:modes, :] = traces_ref[s].astype(jnp.float32) * mode_mask

    eye = lax.broadcasted_iota(jnp.int32, (GRAIN, LANES), 0) == lax.broadcasted_iota(
        jnp.int32, (GRAIN, LANES), 1
    )
    info_out[...] = jnp.zeros_like(info_out)
    for s in range(blocks):
        loads[s].wait()
        for side in range(4):
            links_here = [link for link in links if link[2] == s and link[3] == side]
            for grain in range(grains):
                at = side * face + grain * GRAIN
                block = ops[s, at : at + GRAIN, at : at + GRAIN].astype(jnp.float32)
                block = jnp.where(eye, block, 0.0)
                own_diag[s, at : at + GRAIN, :] = jnp.broadcast_to(
                    jnp.sum(block, axis=1, keepdims=True), (GRAIN, LANES)
                )
                for link in links_here:
                    info_out[link[0], 8 + grain : 9 + grain, :] = jnp.sum(
                        block, axis=0, keepdims=True
                    )
            for link in links_here:
                if side in (EAST, SOUTH):
                    info_out[link[0], 0:8, :] = live[s, side // 2]

    for link in far_links:

        @pl.when(link[4])
        def _(link=link):
            first_arrival(link).wait_recv()

    for link in links:

        @pl.when(link[4])
        def _(link=link):
            plain_copy(*info_bufs, link).start()

    def multiply(s, side, wide):
        columns = 2 * LANES if wide else LANES
        part = jnp.dot(
            ops[s, rows_of(side), :],
            signed[s, :, 0:columns],
            preferred_element_type=jnp.float32,
        )
        if SIGN[side] < 0:
            part = -part
        own_prod[s, rows_of(side), :] = part[:, 0:LANES]
        if wide:
            base_prod[s, rows_of(side), :] = part[:, LANES:]

    def encode(s, side, slot, index):
        product, offset = (base_prod, LANES) if index == base_index else (own_prod, 0)
        for grain in range(grains):
            at = pl.ds(side * face + grain * GRAIN, GRAIN)
            vector = signed[s, at, offset : offset + LANES].astype(jnp.float32) * SIGN[side]
            rest = product[s, at, :] - own_diag[s, at, :] * vector
            largest = jnp.max(jnp.abs(rest), axis=0, keepdims=True)
            inverse = jnp.where(largest > TINY, TOP / jnp.maximum(largest, TINY), 0.0)
            scale_out[index, slot, grain : grain + 1, :] = largest * (1.0 / TOP)
            code_out[index, slot, grain * GRAIN : (grain + 1) * GRAIN, :] = (
                jnp.round(rest * inverse).astype(jnp.int32).astype(jnp.int16)
            )

    def decode(s, side, slot, index, grain):
        product, offset = (base_prod, LANES) if index == base_index else (own_prod, 0)
        at = pl.ds(side * face + grain * GRAIN, GRAIN)
        inner = slice(grain * GRAIN, (grain + 1) * GRAIN)
        vector = signed[s, at, offset : offset + LANES].astype(jnp.float32) * SIGN[side]
        rest = (
            code_in[index, slot, inner, :].astype(jnp.int32).astype(jnp.float32)
            * scale_in[index, slot, grain : grain + 1, :]
        )
        return product[s, at, :] + far_diag[slot, inner, :] * vector + rest

    def send_codes(link, index):
        plain_copy(*scale_bufs, link, index).start()
        plain_copy(*code_bufs, link, index).start()

    def await_codes(link, index):
        arrival(*scale_bufs, link, index).wait_recv()
        arrival(*code_bufs, link, index).wait_recv()

    scale_out[...] = jnp.zeros_like(scale_out)
    sums_out[...] = jnp.zeros_like(sums_out)
    inner_faces = [(s, SOUTH) for s in range(blocks - 1)] + [
        (s, NORTH) for s in range(1, blocks)
    ]

    for sweep in range(ITERS):
        last = sweep == ITERS - 1
        wide = sweep == 0
        for link in links:
            here, _, s, side, cond, _ = link
            multiply(s, side, wide)
            if last and side in (EAST, SOUTH):
                continue

            @pl.when(cond)
            def _(link=link, here=here, s=s, side=side, sweep=sweep):
                encode(s, side, here, sweep)
                send_codes(link, sweep)

        for s, side in inner_faces:
            multiply(s, side, wide)

        if wide:
            for link in far_links:

                @pl.when(link[4])
                def _(link=link):
                    encode(link[2], link[3], link[0], base_index)
                    send_codes(link, base_index)

            for s in range(blocks):
                gap = jnp.dot(
                    traces_own[s].astype(jnp.bfloat16),
                    signed[s, :, LANES : 2 * LANES],
                    preferred_element_type=jnp.float32,
                )
                masked_rhs = coarse_rhs_ref[s] * coarse_live[s]
                targets = [link for link in far_links if link[2] == s]
                modes_own = modes_out.at[2 * blocks + 2 + s]
                modes_own[...] = jnp.zeros_like(modes_own)
                modes_own[0:modes, :] = coarse_mult_ref[s] * coarse_live[s]
                modes_own[MODE_ROWS : MODE_ROWS + modes, :] = gap[0:modes, :] - masked_rhs
                for link in targets:
                    here, side = link[0], link[3]
                    modes_out[here, 0 : 2 * MODE_ROWS, :] = modes_own[0 : 2 * MODE_ROWS, :]
                    for grain in range(grains):
                        at = side * face + grain * GRAIN
                        base_row = (2 + grain) * MODE_ROWS
                        modes_out[here, base_row : base_row + MODE_ROWS, :] = traces_own[
                            s, :, at : at + GRAIN
                        ]
            for link in far_links:

                @pl.when(link[4])
                def _(link=link):
                    plain_copy(*modes_bufs, link).start()

            for link in links:

                @pl.when(link[4])
                def _(link=link):
                    here = link[0]
                    arrival(*info_bufs, link).wait_recv()
                    for grain in range(grains):
                        line = info_in[here, 8 + grain : 9 + grain, :]
                        line = jnp.where(eye, jnp.broadcast_to(line, (GRAIN, LANES)), 0.0)
                        far_diag[here, grain * GRAIN : (grain + 1) * GRAIN, :] = (
                            jnp.broadcast_to(
                                jnp.sum(line, axis=1, keepdims=True), (GRAIN, LANES)
                            )
                        )

        def finish(s, side, grain, value, sweep=sweep, last=last):
            at = pl.ds(side * face + grain * GRAIN, GRAIN)
            if not last:
                signed[s, at, 0:LANES] = (value * SIGN[side]).astype(jnp.bfloat16)
            if side in (EAST, SOUTH):
                if sweep >= ITERS - 2:
                    total_row = sweep - (ITERS - 2)
                    sums_out[0, total_row : total_row + 1, :] += jnp.sum(
                        value * value, axis=0, keepdims=True
                    )
                if last:
                    out_at = pl.ds((side // 2) * face + grain * GRAIN, GRAIN)
                    power_ref[s, out_at, :] = value

        for s in range(blocks - 1):
            for grain in range(grains):
                mask = live[s, 1, grain : grain + 1, :]
                upper = pl.ds(SOUTH * face + grain * GRAIN, GRAIN)
                lower = pl.ds(NORTH * face + grain * GRAIN, GRAIN)
                value = (own_prod[s, upper, :] + own_prod[s + 1, lower, :]) * mask
                finish(s, SOUTH, grain, value)
                if not last:
                    finish(s + 1, NORTH, grain, value)
                if wide:
                    base_grad[s, pl.ds(face + grain * GRAIN, GRAIN), :] = (
                        base_prod[s, upper, :] + base_prod[s + 1, lower, :]
                    )

        for link in links:
            here, _, s, side, cond, _ = link
            if last and side in (WEST, NORTH):
                continue

            @pl.when(cond)
            def _(link=link, here=here, s=s, side=side, sweep=sweep, finish=finish):
                await_codes(link, sweep)
                for grain in range(grains):
                    if side in (EAST, SOUTH):
                        mask = live[s, side // 2, grain : grain + 1, :]
                    else:
                        mask = info_in[here, grain : grain + 1, :]
                    finish(s, side, grain, decode(s, side, here, sweep, grain) * mask)

    sums_col[col] = sums_out[0]
    col_copies = []
    for step in range(1, mesh_cols):
        copy = remote(
            sums_out.at[0],
            sums_col.at[col],
            col_send.at[step],
            col_recv.at[step],
            (row, lax.rem(col + step, mesh_cols)),
        )
        copy.start()
        col_copies.append(copy)

    for link in owner_links:

        @pl.when(link[4])
        def _(link=link):
            here, _, s, side = link[:4]
            await_codes(link, base_index)
            arrival(*modes_bufs, link).wait_recv()
            for grain in range(grains):
                out_at = pl.ds((side // 2) * face + grain * GRAIN, GRAIN)
                base_grad[s, out_at, :] = decode(s, side, here, base_index, grain)

    for copy in col_copies:
        copy.wait()
    sums_out[1] = jnp.sum(sums_col[...], axis=0)
    sums_row[row] = sums_out[1]
    row_copies = []
    for step in range(1, mesh_rows):
        copy = remote(
            sums_out.at[1],
            sums_row.at[row],
            row_send.at[step],
            row_recv.at[step],
            (lax.rem(row + step, mesh_rows), col),
        )
        copy.start()
        row_copies.append(copy)
    for copy in row_copies:
        copy.wait()
    totals = jnp.sum(sums_row[...], axis=0)
    previous = totals[0:1, :]
    newest = totals[1:2, :]
    column_norms = jnp.sqrt((newest + EPSILON) / (previous + EPSILON))
    norms_ref[...] = column_norms
    penalty = jnp.max(column_norms, axis=1, keepdims=True)
    step_length = 1.9 / penalty
    inverse_norm = 1.0 / jnp.sqrt(newest + EPSILON)

    def coefficients(buf):
        return buf[0:MODE_ROWS, :] + penalty * buf[MODE_ROWS : 2 * MODE_ROWS, :]

    own_coarse = [coefficients(modes_out.at[2 * blocks + 2 + s]) for s in range(blocks)]
    for s in range(blocks):
        new_coarse_ref[s] = own_coarse[s][0:modes, :]
    for s in range(blocks):
        for half, side in ((0, EAST), (1, SOUTH)):
            slot = blocks + s if side == EAST else south_slot
            local = side == SOUTH and s < blocks - 1
            far_coarse = own_coarse[s + 1] if local else coefficients(modes_in.at[slot])
            pair = jnp.concatenate([own_coarse[s], far_coarse], axis=0)
            hit = (contact_ref[s, half] > 0).astype(jnp.float32)
            for grain in range(grains):
                at = side * face + grain * GRAIN
                if local:
                    far_at = at - face
                    far_traces = traces_own[s + 1, :, far_at : far_at + GRAIN]
                else:
                    base_row = (2 + grain) * MODE_ROWS
                    far_traces = modes_in[slot, base_row : base_row + MODE_ROWS, :]
                both = jnp.concatenate(
                    [traces_own[s, :, at : at + GRAIN], -far_traces], axis=0
                )
                coarse_part = lax.dot_general(
                    both,
                    pair,
                    (((0,), (0,)), ((), ())),
                    precision=lax.Precision.HIGHEST,
                    preferred_element_type=jnp.float32,
                )
                out_at = pl.ds(half * face + grain * GRAIN, GRAIN)
                mask = live[s, half, grain : grain + 1, :]
                grad = (base_grad[s, out_at, :] + coarse_part - rhs_ref[s, out_at, :]) * mask
                trial = mult_ref[s, out_at, :] * mask - step_length * grad
                clipped = jnp.maximum(trial, 0.0)
                new_mult_ref[s, out_at, :] = jnp.where(hit > 0.0, clipped, trial) * mask
                power_ref[s, out_at, :] = power_ref[s, out_at, :] * inverse_norm

    for link in links:
        owner = link[3] in (EAST, SOUTH)

        @pl.when(link[4])
        def _(link=link, owner=owner):
            plain_copy(*info_bufs, link).wait_send()
            indices = list(range(ITERS - 1)) if owner else list(range(ITERS + 1))
            for index in indices:
                plain_copy(*scale_bufs, link, index).wait_send()
                plain_copy(*code_bufs, link, index).wait_send()
            if owner:
                first_copy(link).wait_send()
            else:
                plain_copy(*modes_bufs, link).wait_send()


def body(
    mesh_rows,
    mesh_cols,
    local_ops,
    start_vecs,
    multipliers,
    dual_rhs,
    mode_traces,
    coarse_mult,
    coarse_rhs,
    face_size,
    contact,
    mode_count,
):
    blocks = local_ops.shape[0]
    order_size = local_ops.shape[2]
    owned_len = start_vecs.shape[2]
    columns = start_vecs.shape[3]
    face = owned_len // 2
    modes = mode_traces.shape[2]
    slots = 2 * blocks + 2
    mode_height = (2 + face // GRAIN) * MODE_ROWS
    vmem = pl.BlockSpec(memory_space=pltpu.VMEM)
    smem = pl.BlockSpec(memory_space=pltpu.SMEM)
    dma = pltpu.SemaphoreType.DMA
    f32, bf16, i16 = jnp.float32, jnp.bfloat16, jnp.int16
    flops = 2 * blocks * order_size * order_size * columns * (ITERS + 1)
    new_mult, power, norms, new_coarse = pl.pallas_call(
        functools.partial(kernel, mesh_rows, mesh_cols),
        out_shape=(
            jax.ShapeDtypeStruct((blocks, owned_len, columns), f32),
            jax.ShapeDtypeStruct((blocks, owned_len, columns), f32),
            jax.ShapeDtypeStruct((1, columns), f32),
            jax.ShapeDtypeStruct((blocks, modes, columns), f32),
        ),
        in_specs=[pl.BlockSpec(memory_space=pl.ANY)] + [vmem] * 6 + [smem] * 3,
        out_specs=(vmem, vmem, vmem, vmem),
        scratch_shapes=[
            pltpu.VMEM((blocks, order_size, order_size), bf16),
            pltpu.VMEM((blocks, order_size, 2 * columns), bf16),
            pltpu.VMEM((slots, face, 2 * columns), bf16),
            pltpu.VMEM((blocks, order_size, columns), f32),
            pltpu.VMEM((blocks, order_size, columns), f32),
            pltpu.VMEM((blocks, owned_len, columns), f32),
            pltpu.VMEM((blocks, order_size, columns), f32),
            pltpu.VMEM((slots, face, columns), f32),
            pltpu.VMEM((slots, 16, columns), f32),
            pltpu.VMEM((slots, 16, columns), f32),
            pltpu.VMEM((ITERS + 1, slots, face, columns), i16),
            pltpu.VMEM((ITERS + 1, slots, face, columns), i16),
            pltpu.VMEM((ITERS + 1, slots, 8, columns), f32),
            pltpu.VMEM((ITERS + 1, slots, 8, columns), f32),
            pltpu.VMEM((slots + blocks, mode_height, columns), f32),
            pltpu.VMEM((slots, mode_height, columns), f32),
            pltpu.VMEM((blocks, MODE_ROWS, order_size), f32),
            pltpu.VMEM((blocks, 2, 8, columns), f32),
            pltpu.VMEM((2, 8, columns), f32),
            pltpu.VMEM((mesh_cols, 8, columns), f32),
            pltpu.VMEM((mesh_rows, 8, columns), f32),
            dma((blocks,)),
            dma((slots,)),
            dma((slots,)),
            dma((slots,)),
            dma((slots,)),
            dma((ITERS + 1, slots)),
            dma((ITERS + 1, slots)),
            dma((ITERS + 1, slots)),
            dma((ITERS + 1, slots)),
            dma((slots,)),
            dma((slots,)),
            dma((mesh_cols,)),
            dma((mesh_cols,)),
            dma((mesh_rows,)),
            dma((mesh_rows,)),
        ],
        compiler_params=pltpu.CompilerParams(
            collective_id=0, has_side_effects=True, vmem_limit_bytes=56 * 1024 * 1024
        ),
        cost_estimate=pl.CostEstimate(
            flops=flops, bytes_accessed=2 * blocks * order_size * order_size, transcendentals=0
        ),
    )(
        local_ops.reshape(blocks, order_size, order_size),
        start_vecs.reshape(blocks, owned_len, columns),
        multipliers.reshape(blocks, owned_len, columns),
        dual_rhs.reshape(blocks, owned_len, columns),
        mode_traces.reshape(blocks, modes, order_size),
        coarse_mult.reshape(blocks, modes, columns),
        coarse_rhs.reshape(blocks, modes, columns),
        face_size.reshape(blocks, 2),
        contact.reshape(blocks, 2),
        mode_count.reshape(blocks, 1),
    )
    return (
        new_mult.reshape(blocks, 1, owned_len, columns),
        power.reshape(blocks, 1, owned_len, columns),
        norms.reshape(columns),
        new_coarse.reshape(blocks, 1, modes, columns),
    )


def solution(mesh):
    wide = P("row", "col", None, None)
    sizes = dict(mesh.shape)
    return jax.shard_map(
        functools.partial(body, sizes["row"], sizes["col"]),
        mesh=mesh,
        in_specs=(wide,) * 7 + (P("row", "col", None), P("row", "col", None), P("row", "col")),
        out_specs=(wide, wide, P(), wide),
        check_vma=False,
    )
```

```python
import functools
import jax
import jax.numpy as jnp
from jax import lax
from jax.experimental import pallas as pl
from jax.experimental.pallas import tpu as pltpu
from jax.sharding import PartitionSpec as P

ITERS = 4
EPSILON = 1e-06
LANES = 128
GRAIN = 128
MODE_ROWS = 8
TOP = 32767.0
TINY = 1e-30
WEST, EAST, NORTH, SOUTH = 0, 1, 2, 3
SIGN = (-1.0, 1.0, -1.0, 1.0)
MESH = pl.DeviceIdType.MESH


def kernel(
    mesh_rows,
    mesh_cols,
    ops_hbm,
    start_ref,
    mult_ref,
    rhs_ref,
    traces_ref,
    coarse_mult_ref,
    coarse_rhs_ref,
    size_ref,
    contact_ref,
    count_ref,
    new_mult_ref,
    power_ref,
    norms_ref,
    new_coarse_ref,
    ops,
    signed,
    first_out,
    own_prod,
    base_prod,
    base_grad,
    gap_grad,
    own_diag,
    far_diag,
    info_out,
    info_in,
    code_out,
    code_in,
    scale_out,
    scale_in,
    modes_out,
    modes_in,
    traces_own,
    live,
    sums_out,
    sums_col,
    sums_row,
    load_sems,
    first_send,
    first_recv,
    info_send,
    info_recv,
    code_send,
    code_recv,
    scale_send,
    scale_recv,
    modes_send,
    modes_recv,
    col_send,
    col_recv,
    row_send,
    row_recv,
):
    blocks, order_size, _ = ops.shape
    face = order_size // 4
    grains = face // GRAIN
    modes = traces_ref.shape[1]
    base_index = ITERS
    row = lax.axis_index("row")
    col = lax.axis_index("col")

    loads = [
        pltpu.make_async_copy(ops_hbm.at[s], ops.at[s], load_sems.at[s]) for s in range(blocks)
    ]
    for load in loads:
        load.start()

    barrier = pltpu.get_barrier_semaphore()
    for step in range(1, mesh_cols):
        pl.semaphore_signal(
            barrier,
            inc=1,
            device_id=(row, lax.rem(col + step, mesh_cols)),
            device_id_type=MESH,
        )
    for step in range(1, mesh_rows):
        pl.semaphore_signal(
            barrier,
            inc=1,
            device_id=(lax.rem(row + step, mesh_rows), col),
            device_id_type=MESH,
        )

    links = []
    for s in range(blocks):
        links.append((s, blocks + s, s, WEST, col > 0, (row, col - 1)))
        links.append((blocks + s, s, s, EAST, col < mesh_cols - 1, (row, col + 1)))
    north_slot, south_slot = 2 * blocks, 2 * blocks + 1
    links.append((north_slot, south_slot, 0, NORTH, row > 0, (row - 1, col)))
    links.append(
        (south_slot, north_slot, blocks - 1, SOUTH, row < mesh_rows - 1, (row + 1, col))
    )
    owner_links = [link for link in links if link[3] in (EAST, SOUTH)]
    far_links = [link for link in links if link[3] in (WEST, NORTH)]

    def rows_of(side):
        return pl.ds(side * face, face)

    def remote(src, dst, send_sem, recv_sem, device):
        return pltpu.make_async_remote_copy(
            src_ref=src,
            dst_ref=dst,
            send_sem=send_sem,
            recv_sem=recv_sem,
            device_id=device,
            device_id_type=MESH,
        )

    def first_copy(link, group):
        here, there, s, side, _, device = link
        far_s = s if side == EAST else 0
        return remote(
            first_out.at[group, here],
            signed.at[far_s, rows_of(side - 1), pl.ds(group * LANES, LANES)],
            first_send.at[group, here],
            first_recv.at[group, there],
            device,
        )

    def first_arrival(link, group):
        here, _, s, side, _, device = link
        return remote(
            first_out.at[group, here],
            signed.at[s, rows_of(side), pl.ds(group * LANES, LANES)],
            first_send.at[group, here],
            first_recv.at[group, here],
            device,
        )

    def plain_copy(src, dst, send_sems, recv_sems, link, index=None):
        here, there, device = link[0], link[1], link[5]
        if index is None:
            return remote(
                src.at[here], dst.at[there], send_sems.at[here], recv_sems.at[there], device
            )
        return remote(
            src.at[index, here],
            dst.at[index, there],
            send_sems.at[index, here],
            recv_sems.at[index, there],
            device,
        )

    def arrival(src, dst, send_sems, recv_sems, link, index=None):
        here, device = link[0], link[5]
        if index is None:
            return remote(
                src.at[here], dst.at[here], send_sems.at[here], recv_sems.at[here], device
            )
        return remote(
            src.at[index, here],
            dst.at[index, here],
            send_sems.at[index, here],
            recv_sems.at[index, here],
            device,
        )

    info_bufs = (info_out, info_in, info_send, info_recv)
    code_bufs = (code_out, code_in, code_send, code_recv)
    scale_bufs = (scale_out, scale_in, scale_send, scale_recv)
    modes_bufs = (modes_out, modes_in, modes_send, modes_recv)

    grain_start = lax.broadcasted_iota(jnp.int32, (8, LANES), 0) * GRAIN
    for s in range(blocks):
        for half in range(2):
            live[s, half] = (grain_start < size_ref[s, half]).astype(jnp.float32)
    for s in range(blocks):
        for half, side in ((0, EAST), (1, SOUTH)):
            for grain in range(grains):
                mask = live[s, half, grain : grain + 1, :]
                src = pl.ds(half * face + grain * GRAIN, GRAIN)
                dst = pl.ds(side * face + grain * GRAIN, GRAIN)
                signed[s, dst, 0:LANES] = (start_ref[s, src, :] * mask).astype(jnp.bfloat16)
                signed[s, dst, LANES : 2 * LANES] = (mult_ref[s, src, :] * mask).astype(
                    jnp.bfloat16
                )
    for link in owner_links:
        here, _, s, side = link[:4]
        for group in range(2):
            first_out[group, here] = -signed[
                s, rows_of(side), group * LANES : (group + 1) * LANES
            ]
    for s in range(1, blocks):
        signed[s, rows_of(NORTH), :] = -signed[s - 1, rows_of(SOUTH), :]

    pl.semaphore_wait(barrier, mesh_cols - 1 + mesh_rows - 1)
    for link in owner_links:

        @pl.when(link[4])
        def _(link=link):
            first_copy(link, 0).start()

    for link in far_links:

        @pl.when(jnp.logical_not(link[4]))
        def _(link=link):
            signed[link[2], rows_of(link[3]), :] = jnp.zeros((face, 2 * LANES), jnp.bfloat16)

    for link in owner_links:

        @pl.when(jnp.logical_not(link[4]))
        def _(link=link):
            here, _, s, side = link[:4]
            modes_in[here] = jnp.zeros(modes_in.shape[1:], jnp.float32)
            out_rows = pl.ds((side // 2) * face, face)
            power_ref[s, out_rows, :] = jnp.zeros((face, LANES), jnp.float32)
            base_grad[s, out_rows, :] = jnp.zeros((face, LANES), jnp.float32)

    traces_own[...] = jnp.zeros_like(traces_own)
    coarse_live = []
    for s in range(blocks):
        mask = (
            lax.broadcasted_iota(jnp.int32, (modes, LANES), 0) < count_ref[s, 0]
        ).astype(jnp.float32)
        coarse_live.append(mask)
        mode_mask = (
            lax.broadcasted_iota(jnp.int32, (modes, order_size), 0) < count_ref[s, 0]
        ).astype(jnp.float32)
        traces_own[s, 0:modes, :] = traces_ref[s].astype(jnp.float32) * mode_mask

    eye = lax.broadcasted_iota(jnp.int32, (GRAIN, LANES), 0) == lax.broadcasted_iota(
        jnp.int32, (GRAIN, LANES), 1
    )
    info_out[...] = jnp.zeros_like(info_out)
    for s in range(blocks):
        loads[s].wait()
        for side in range(4):
            links_here = [link for link in links if link[2] == s and link[3] == side]
            for grain in range(grains):
                at = side * face + grain * GRAIN
                whole = ops[s, at : at + GRAIN, at : at + GRAIN].astype(jnp.float32)
                block = jnp.where(eye, whole, 0.0)
                ops[s, at : at + GRAIN, at : at + GRAIN] = jnp.where(eye, 0.0, whole).astype(
                    jnp.bfloat16
                )
                own_diag[s, at : at + GRAIN, :] = jnp.broadcast_to(
                    jnp.sum(block, axis=1, keepdims=True), (GRAIN, LANES)
                )
                for link in links_here:
                    info_out[link[0], 8 + grain : 9 + grain, :] = jnp.sum(
                        block, axis=0, keepdims=True
                    )
            for link in links_here:
                if side in (EAST, SOUTH):
                    info_out[link[0], 0:8, :] = live[s, side // 2]

    for link in far_links:

        @pl.when(link[4])
        def _(link=link):
            first_arrival(link, 0).wait_recv()

    for link in links:

        @pl.when(link[4])
        def _(link=link):
            plain_copy(*info_bufs, link).start()

    def multiply(s, side, wide):
        columns = 2 * LANES if wide else LANES
        part = jnp.dot(
            ops[s, rows_of(side), :],
            signed[s, :, 0:columns],
            preferred_element_type=jnp.float32,
        )
        if SIGN[side] < 0:
            part = -part
        own_prod[s, rows_of(side), :] = part[:, 0:LANES]
        if wide:
            base_prod[s, rows_of(side), :] = part[:, LANES:]

    def encode(s, side, slot, index):
        product = base_prod if index == base_index else own_prod
        for grain in range(grains):
            at = pl.ds(side * face + grain * GRAIN, GRAIN)
            rest = product[s, at, :]
            largest = jnp.max(jnp.abs(rest), axis=0, keepdims=True)
            inverse = jnp.where(largest > TINY, TOP / jnp.maximum(largest, TINY), 0.0)
            scale_out[index, slot, grain : grain + 1, :] = largest * (1.0 / TOP)
            code_out[index, slot, grain * GRAIN : (grain + 1) * GRAIN, :] = (
                jnp.round(rest * inverse).astype(jnp.int32).astype(jnp.int16)
            )

    def decode(s, side, slot, index, grain):
        product, offset = (base_prod, LANES) if index == base_index else (own_prod, 0)
        at = pl.ds(side * face + grain * GRAIN, GRAIN)
        inner = slice(grain * GRAIN, (grain + 1) * GRAIN)
        vector = signed[s, at, offset : offset + LANES].astype(jnp.float32) * SIGN[side]
        rest = (
            code_in[index, slot, inner, :].astype(jnp.int32).astype(jnp.float32)
            * scale_in[index, slot, grain : grain + 1, :]
        )
        return product[s, at, :] + far_diag[slot, inner, :] * vector + rest

    def send_codes(link, index):
        plain_copy(*scale_bufs, link, index).start()
        plain_copy(*code_bufs, link, index).start()

    def await_codes(link, index):
        arrival(*scale_bufs, link, index).wait_recv()
        arrival(*code_bufs, link, index).wait_recv()

    scale_out[...] = jnp.zeros_like(scale_out)
    sums_out[...] = jnp.zeros_like(sums_out)
    inner_faces = [(s, SOUTH) for s in range(blocks - 1)] + [
        (s, NORTH) for s in range(1, blocks)
    ]

    def finish(s, side, grain, value, sweep):
        at = pl.ds(side * face + grain * GRAIN, GRAIN)
        if sweep < ITERS - 1:
            signed[s, at, 0:LANES] = (value * SIGN[side]).astype(jnp.bfloat16)
        if side in (EAST, SOUTH):
            if sweep >= ITERS - 2:
                total_row = sweep - (ITERS - 2)
                sums_out[0, total_row : total_row + 1, :] += jnp.sum(
                    value * value, axis=0, keepdims=True
                )
            if sweep == ITERS - 1:
                out_at = pl.ds((side // 2) * face + grain * GRAIN, GRAIN)
                power_ref[s, out_at, :] = value

    def finish_inner(sweep):
        for s in range(blocks - 1):
            for grain in range(grains):
                mask = live[s, 1, grain : grain + 1, :]
                upper = pl.ds(SOUTH * face + grain * GRAIN, GRAIN)
                lower = pl.ds(NORTH * face + grain * GRAIN, GRAIN)
                both_diag = own_diag[s, upper, :] + own_diag[s + 1, lower, :]
                vector = signed[s, upper, 0:LANES].astype(jnp.float32)
                value = (
                    own_prod[s, upper, :] + own_prod[s + 1, lower, :] + both_diag * vector
                ) * mask
                finish(s, SOUTH, grain, value, sweep)
                if sweep < ITERS - 1:
                    finish(s + 1, NORTH, grain, value, sweep)
                if sweep == ITERS - 2:
                    vector = signed[s, upper, LANES : 2 * LANES].astype(jnp.float32)
                    base_grad[s, pl.ds(face + grain * GRAIN, GRAIN), :] = (
                        base_prod[s, upper, :] + base_prod[s + 1, lower, :] + both_diag * vector
                    )

    def drain(sweep, block):
        for link in links:
            here, _, s, side, cond, _ = link
            if s != block or (sweep == ITERS - 1 and side in (WEST, NORTH)):
                continue

            @pl.when(cond)
            def _(link=link, here=here, s=s, side=side):
                await_codes(link, sweep)
                for grain in range(grains):
                    if side in (EAST, SOUTH):
                        mask = live[s, side // 2, grain : grain + 1, :]
                    else:
                        mask = info_in[here, grain : grain + 1, :]
                    finish(s, side, grain, decode(s, side, here, sweep, grain) * mask, sweep)

    def finish_base():
        for link in owner_links:

            @pl.when(link[4])
            def _(link=link):
                here, _, s, side = link[:4]
                await_codes(link, base_index)
                arrival(*modes_bufs, link).wait_recv()
                for grain in range(grains):
                    out_at = pl.ds((side // 2) * face + grain * GRAIN, GRAIN)
                    base_grad[s, out_at, :] = decode(s, side, here, base_index, grain)

        def coefficients(buf):
            return jnp.concatenate(
                [buf[0:MODE_ROWS, :], buf[MODE_ROWS : 2 * MODE_ROWS, :]], axis=1
            )

        own_coarse = [coefficients(modes_out.at[2 * blocks + 2 + s]) for s in range(blocks)]
        for s in range(blocks):
            for half, side in ((0, EAST), (1, SOUTH)):
                slot = blocks + s if side == EAST else south_slot
                if side == SOUTH and s < blocks - 1:
                    far_coarse = own_coarse[s + 1]
                    far_traces = traces_own[s + 1, :, (side - 1) * face : side * face]
                else:
                    far_coarse = coefficients(modes_in.at[slot])
                    far_traces = jnp.concatenate(
                        [
                            modes_in[slot, (2 + grain) * MODE_ROWS : (3 + grain) * MODE_ROWS, :]
                            for grain in range(grains)
                        ],
                        axis=1,
                    )
                own_traces = traces_own[s, :, side * face : (side + 1) * face]
                part = lax.dot_general(
                    jnp.concatenate([own_traces, -far_traces], axis=0),
                    jnp.concatenate([own_coarse[s], far_coarse], axis=0),
                    (((0,), (0,)), ((), ())),
                    precision=lax.Precision.HIGHEST,
                    preferred_element_type=jnp.float32,
                )
                for grain in range(grains):
                    inner = slice(grain * GRAIN, (grain + 1) * GRAIN)
                    out_at = pl.ds(half * face + grain * GRAIN, GRAIN)
                    mask = live[s, half, grain : grain + 1, :]
                    base_grad[s, out_at, :] = (
                        base_grad[s, out_at, :] + part[inner, 0:LANES] - rhs_ref[s, out_at, :]
                    ) * mask
                    gap_grad[s, out_at, :] = part[inner, LANES:] * mask

    for sweep in range(ITERS):
        last = sweep == ITERS - 1
        wide = sweep == ITERS - 2
        if wide:
            for link in far_links:

                @pl.when(link[4])
                def _(link=link):
                    first_arrival(link, 1).wait_recv()

        if sweep > 0:
            finish_inner(sweep - 1)
        for s in range(blocks):
            if sweep > 0:
                drain(sweep - 1, s)
            ordered = [link for link in (far_links if last else links) if link[2] == s]
            waiting = None
            for link in ordered + [None]:
                if link is not None:
                    multiply(s, link[3], wide)
                if waiting is not None:
                    encode(s, waiting[3], waiting[0], sweep)

                    @pl.when(waiting[4])
                    def _(link=waiting, sweep=sweep):
                        send_codes(link, sweep)

                waiting = link
            for link in owner_links if last else []:
                if link[2] == s:
                    multiply(s, link[3], wide)
            for inner_s, side in inner_faces:
                if inner_s == s:
                    multiply(s, side, wide)
        if sweep == 0:
            for link in owner_links:

                @pl.when(link[4])
                def _(link=link):
                    first_copy(link, 1).start()

        if wide:
            for link in far_links:

                @pl.when(link[4])
                def _(link=link):
                    encode(link[2], link[3], link[0], base_index)
                    send_codes(link, base_index)

            for s in range(blocks):
                gap = jnp.dot(
                    traces_own[s].astype(jnp.bfloat16),
                    signed[s, :, LANES : 2 * LANES],
                    preferred_element_type=jnp.float32,
                )
                masked_rhs = coarse_rhs_ref[s] * coarse_live[s]
                targets = [link for link in far_links if link[2] == s]
                modes_own = modes_out.at[2 * blocks + 2 + s]
                modes_own[...] = jnp.zeros_like(modes_own)
                modes_own[0:modes, :] = coarse_mult_ref[s] * coarse_live[s]
                modes_own[MODE_ROWS : MODE_ROWS + modes, :] = gap[0:modes, :] - masked_rhs
                for link in targets:
                    here, side = link[0], link[3]
                    modes_out[here, 0 : 2 * MODE_ROWS, :] = modes_own[0 : 2 * MODE_ROWS, :]
                    for grain in range(grains):
                        at = side * face + grain * GRAIN
                        base_row = (2 + grain) * MODE_ROWS
                        modes_out[here, base_row : base_row + MODE_ROWS, :] = traces_own[
                            s, :, at : at + GRAIN
                        ]
            for link in far_links:

                @pl.when(link[4])
                def _(link=link):
                    plain_copy(*modes_bufs, link).start()

        if sweep == 0:
            for link in links:

                @pl.when(link[4])
                def _(link=link):
                    here = link[0]
                    arrival(*info_bufs, link).wait_recv()
                    for grain in range(grains):
                        line = info_in[here, 8 + grain : 9 + grain, :]
                        line = jnp.where(eye, jnp.broadcast_to(line, (GRAIN, LANES)), 0.0)
                        at = pl.ds(link[3] * face + grain * GRAIN, GRAIN)
                        far_diag[here, grain * GRAIN : (grain + 1) * GRAIN, :] = (
                            own_diag[link[2], at, :] + jnp.sum(line, axis=1, keepdims=True)
                        )

    finish_base()
    finish_inner(ITERS - 1)
    for s in range(blocks):
        drain(ITERS - 1, s)

    sums_col[col] = sums_out[0]
    col_copies = []
    for step in range(1, mesh_cols):
        copy = remote(
            sums_out.at[0],
            sums_col.at[col],
            col_send.at[step],
            col_recv.at[step],
            (row, lax.rem(col + step, mesh_cols)),
        )
        copy.start()
        col_copies.append(copy)

    for copy in col_copies:
        copy.wait()
    sums_out[1] = jnp.sum(sums_col[...], axis=0)
    sums_row[row] = sums_out[1]
    row_copies = []
    for step in range(1, mesh_rows):
        copy = remote(
            sums_out.at[1],
            sums_row.at[row],
            row_send.at[step],
            row_recv.at[step],
            (lax.rem(row + step, mesh_rows), col),
        )
        copy.start()
        row_copies.append(copy)
    for copy in row_copies:
        copy.wait()
    totals = jnp.sum(sums_row[...], axis=0)
    previous = totals[0:1, :]
    newest = totals[1:2, :]
    column_norms = jnp.sqrt((newest + EPSILON) / (previous + EPSILON))
    norms_ref[...] = column_norms
    penalty = jnp.max(column_norms, axis=1, keepdims=True)
    step_length = 1.9 / penalty
    inverse_norm = 1.0 / jnp.sqrt(newest + EPSILON)

    for s in range(blocks):
        buf = modes_out.at[2 * blocks + 2 + s]
        new_coarse_ref[s] = (
            buf[0:modes, :] + penalty * buf[MODE_ROWS : MODE_ROWS + modes, :]
        )
    for s in range(blocks):
        for half in range(2):
            hit = (contact_ref[s, half] > 0).astype(jnp.float32)
            for grain in range(grains):
                out_at = pl.ds(half * face + grain * GRAIN, GRAIN)
                mask = live[s, half, grain : grain + 1, :]
                grad = base_grad[s, out_at, :] + penalty * gap_grad[s, out_at, :]
                trial = mult_ref[s, out_at, :] * mask - step_length * grad
                clipped = jnp.maximum(trial, 0.0)
                new_mult_ref[s, out_at, :] = jnp.where(hit > 0.0, clipped, trial) * mask
                power_ref[s, out_at, :] = power_ref[s, out_at, :] * inverse_norm

    for link in links:
        owner = link[3] in (EAST, SOUTH)

        @pl.when(link[4])
        def _(link=link, owner=owner):
            plain_copy(*info_bufs, link).wait_send()
            indices = list(range(ITERS - 1)) if owner else list(range(ITERS + 1))
            for index in indices:
                plain_copy(*scale_bufs, link, index).wait_send()
                plain_copy(*code_bufs, link, index).wait_send()
            if owner:
                first_copy(link, 0).wait_send()
                first_copy(link, 1).wait_send()
            else:
                plain_copy(*modes_bufs, link).wait_send()


def body(
    mesh_rows,
    mesh_cols,
    local_ops,
    start_vecs,
    multipliers,
    dual_rhs,
    mode_traces,
    coarse_mult,
    coarse_rhs,
    face_size,
    contact,
    mode_count,
):
    blocks = local_ops.shape[0]
    order_size = local_ops.shape[2]
    owned_len = start_vecs.shape[2]
    columns = start_vecs.shape[3]
    face = owned_len // 2
    modes = mode_traces.shape[2]
    slots = 2 * blocks + 2
    mode_height = (2 + face // GRAIN) * MODE_ROWS
    vmem = pl.BlockSpec(memory_space=pltpu.VMEM)
    smem = pl.BlockSpec(memory_space=pltpu.SMEM)
    dma = pltpu.SemaphoreType.DMA
    f32, bf16, i16 = jnp.float32, jnp.bfloat16, jnp.int16
    flops = 2 * blocks * order_size * order_size * columns * (ITERS + 1)
    new_mult, power, norms, new_coarse = pl.pallas_call(
        functools.partial(kernel, mesh_rows, mesh_cols),
        out_shape=(
            jax.ShapeDtypeStruct((blocks, owned_len, columns), f32),
            jax.ShapeDtypeStruct((blocks, owned_len, columns), f32),
            jax.ShapeDtypeStruct((1, columns), f32),
            jax.ShapeDtypeStruct((blocks, modes, columns), f32),
        ),
        in_specs=[pl.BlockSpec(memory_space=pl.ANY)] + [vmem] * 6 + [smem] * 3,
        out_specs=(vmem, vmem, vmem, vmem),
        scratch_shapes=[
            pltpu.VMEM((blocks, order_size, order_size), bf16),
            pltpu.VMEM((blocks, order_size, 2 * columns), bf16),
            pltpu.VMEM((2, slots, face, columns), bf16),
            pltpu.VMEM((blocks, order_size, columns), f32),
            pltpu.VMEM((blocks, order_size, columns), f32),
            pltpu.VMEM((blocks, owned_len, columns), f32),
            pltpu.VMEM((blocks, owned_len, columns), f32),
            pltpu.VMEM((blocks, order_size, columns), f32),
            pltpu.VMEM((slots, face, columns), f32),
            pltpu.VMEM((slots, 16, columns), f32),
            pltpu.VMEM((slots, 16, columns), f32),
            pltpu.VMEM((ITERS + 1, slots, face, columns), i16),
            pltpu.VMEM((ITERS + 1, slots, face, columns), i16),
            pltpu.VMEM((ITERS + 1, slots, 8, columns), f32),
            pltpu.VMEM((ITERS + 1, slots, 8, columns), f32),
            pltpu.VMEM((slots + blocks, mode_height, columns), f32),
            pltpu.VMEM((slots, mode_height, columns), f32),
            pltpu.VMEM((blocks, MODE_ROWS, order_size), f32),
            pltpu.VMEM((blocks, 2, 8, columns), f32),
            pltpu.VMEM((2, 8, columns), f32),
            pltpu.VMEM((mesh_cols, 8, columns), f32),
            pltpu.VMEM((mesh_rows, 8, columns), f32),
            dma((blocks,)),
            dma((2, slots)),
            dma((2, slots)),
            dma((slots,)),
            dma((slots,)),
            dma((ITERS + 1, slots)),
            dma((ITERS + 1, slots)),
            dma((ITERS + 1, slots)),
            dma((ITERS + 1, slots)),
            dma((slots,)),
            dma((slots,)),
            dma((mesh_cols,)),
            dma((mesh_cols,)),
            dma((mesh_rows,)),
            dma((mesh_rows,)),
        ],
        compiler_params=pltpu.CompilerParams(
            collective_id=0, has_side_effects=True, vmem_limit_bytes=56 * 1024 * 1024
        ),
        cost_estimate=pl.CostEstimate(
            flops=flops, bytes_accessed=2 * blocks * order_size * order_size, transcendentals=0
        ),
    )(
        local_ops.reshape(blocks, order_size, order_size),
        start_vecs.reshape(blocks, owned_len, columns),
        multipliers.reshape(blocks, owned_len, columns),
        dual_rhs.reshape(blocks, owned_len, columns),
        mode_traces.reshape(blocks, modes, order_size),
        coarse_mult.reshape(blocks, modes, columns),
        coarse_rhs.reshape(blocks, modes, columns),
        face_size.reshape(blocks, 2),
        contact.reshape(blocks, 2),
        mode_count.reshape(blocks, 1),
    )
    return (
        new_mult.reshape(blocks, 1, owned_len, columns),
        power.reshape(blocks, 1, owned_len, columns),
        norms.reshape(columns),
        new_coarse.reshape(blocks, 1, modes, columns),
    )


def solution(mesh):
    wide = P("row", "col", None, None)
    sizes = dict(mesh.shape)
    return jax.shard_map(
        functools.partial(body, sizes["row"], sizes["col"]),
        mesh=mesh,
        in_specs=(wide,) * 7 + (P("row", "col", None), P("row", "col", None), P("row", "col")),
        out_specs=(wide, wide, P(), wide),
        check_vma=False,
    )
```
